1024 devices in a mesh: group: 32 (over z, core), mp: 32 (over x, y).
Axes of the slice: x: 4, y: 8, z: 16, core: 2. Of those that a mesh axis runs over, the one named last changes fastest.
Arguments:
- base_rows: bfloat16 [16384, 16384], P('group', 'mp'), may hold values from -6 to 6
- cotangent: bfloat16 [16384, 16384], P('group', 'mp'), may hold values from -6 to 6
- in_panels: bfloat16 [32, 32, 512, 256], P(None, 'mp', 'group'), may hold values from -0.046875 to 0.046875
- out_panels: bfloat16 [32, 32, 512, 256], P(None, 'mp', 'group'), may hold values from -0.375 to 0.375
- gating_weight_matrix: bfloat16 [16384, 32], P('mp'), may hold values from -0.046875 to 0.046875
- cross_bias: float32 [16384], P('mp'), may hold values from -3 to 3
- dev_experts: int32 [32, 2], replicated, may hold values from 0 to 31, as said below
- block_slot: int32 [128], P('group'), may hold values from 0 to 1
- live_blocks: int32 [32], P('group'), may hold values from 1 to 4, as said below
Outputs:
- d_input: bfloat16 [16384, 16384], P('group', 'mp')
- d_in_panels: bfloat16 [32, 32, 512, 256], P(None, 'mp', 'group')
- d_out_panels: bfloat16 [32, 32, 512, 256], P(None, 'mp', 'group')
The draws below stay inside these ranges and needn't reach their ends.
Inputs may be any that keep to these rules, and one draw needn't show every extreme that they name: `dev_experts`: each row names 2 different experts. `live_blocks`: A group's live blocks are its first ones; the others contribute nothing.
All inputs are finite; a program needn't handle non-finite values.
Results may differ from the reference program's by a relative error of at most 0.0057.
Values may be sent and summed in bfloat16 or wider, within the bound.
A program may use at most 32 MiB of HBM per device.

```python
import jax
import jax.numpy as jnp
from jax import lax

D = 16384
E = 32
R = 256
BLOCK = 128
SLOTS = 2
BLK_DEV = 4
GROUPS = 32
MP_SLICES = 32
SLICE = 512
NBLK = 128
ROWS = 16384


def draw_dev_experts(key, part):
    keys = jax.random.split(key, GROUPS)
    perms = jax.vmap(lambda k: jax.random.permutation(k, E))(keys).astype(jnp.int32)
    chosen = jax.random.randint(jax.random.fold_in(key, 7), (), 0, GROUPS).astype(jnp.int32)
    second = (chosen + 1) % GROUPS
    row_ids = jnp.arange(GROUPS, dtype=jnp.int32)[:, None]
    shifted_high = (perms - perms[:, :1] + E - 1) % E
    shifted_low = (perms - perms[:, :1]) % E
    perms = jnp.where(row_ids == chosen, shifted_high, jnp.where(row_ids == second, shifted_low, perms))
    return perms[:, :SLOTS].astype(jnp.int32)


def draw_live_blocks(key, part):
    counts = jax.random.randint(key, (GROUPS,), 1, BLK_DEV + 1).astype(jnp.int32)
    chosen = jax.random.randint(jax.random.fold_in(key, 3), (), 0, GROUPS).astype(jnp.int32)
    second = (chosen + 1) % GROUPS
    row_ids = jnp.arange(GROUPS, dtype=jnp.int32)
    counts = jnp.where(row_ids == second, 1, counts)
    counts = jnp.where(row_ids == chosen, BLK_DEV, counts)
    return counts.astype(jnp.int32)


def place_ends(result, own_key, low, high):
    longest = result.shape.index(max(result.shape))
    spots = []
    for shift in (0, 1):
        where = [jax.random.randint(jax.random.fold_in(own_key, axis), (), 0, length) for axis, length in enumerate(result.shape)]
        where[longest] = (where[longest] + shift) % result.shape[longest]
        spots.append(tuple(where))
    return result.at[spots[0]].set(low).at[spots[1]].set(high)


def steps_of(key, extent, shards, low, high):
    def one(position, parts):
        draws = jax.random.uniform(jax.random.fold_in(jax.random.fold_in(key, 6), position), (parts,), jnp.float32, low / len(shards), high / len(shards))
        return jnp.repeat(jnp.exp(draws), extent[position] // parts).reshape((-1,) + (1,) * (len(extent) - position - 1))

    loudness = one(*shards[0])
    for cut in shards[1:]:
        loudness = loudness * one(*cut)
    return loudness


def noise(rng, extent, spread, bound, shards=(), kind=jnp.bfloat16):
    values = jax.random.normal(rng, extent, jnp.float32) * spread
    if len(shards) > 0:
        values = steps_of(rng, extent, shards, -0.22, 0.18) * values
    return jnp.clip(values, min=-bound, max=bound).astype(kind)


def setup_inputs(seed: int = 0) -> dict:
    arg_keys = jax.random.split(jax.random.key(seed), 10)
    base_rows = noise(arg_keys[0], (ROWS, D), 1.0, 6.0, ((0, 32), (1, 32)))
    cotangent = noise(arg_keys[1], (ROWS, D), 1.0, 6.0, ((0, 32), (1, 32)))
    in_panels = noise(arg_keys[2], (E, MP_SLICES, SLICE, R), D ** -0.5, 0.046875, ((1, 32), (2, 32)))
    out_panels = noise(arg_keys[3], (E, MP_SLICES, SLICE, R), R ** -0.5, 0.375, ((1, 32), (2, 32)))
    gating_weight_matrix = noise(arg_keys[4], (D, E), D ** -0.5, 0.046875, ((0, 32),))
    cross_bias = noise(arg_keys[5], (D,), 0.5, 3.0, ((0, 32),), jnp.float32)
    dev_experts = draw_dev_experts(jax.random.fold_in(arg_keys[9], 71), 0)
    block_slot = place_ends(jax.random.randint(arg_keys[7], (NBLK,), 0, SLOTS), jax.random.fold_in(arg_keys[7], 1), 0, SLOTS - 1).astype(jnp.int32)
    live_blocks = draw_live_blocks(jax.random.fold_in(arg_keys[9], 71), 0)
    return dict(base_rows=base_rows, cotangent=cotangent, in_panels=in_panels, out_panels=out_panels, gating_weight_matrix=gating_weight_matrix, cross_bias=cross_bias, dev_experts=dev_experts, block_slot=block_slot, live_blocks=live_blocks)


def reference(base_rows, cotangent, in_panels, out_panels, gating_weight_matrix, cross_bias, dev_experts, block_slot, live_blocks):
    in_all = in_panels.reshape(E, D, R)
    out_all = out_panels.reshape(E, D, R)

    def step(carry, index):
        grad_in, grad_out = carry
        group_id = index // BLK_DEV
        place = index % BLK_DEV
        live_flag = (place < live_blocks[group_id]).astype(jnp.float32)
        expert = dev_experts[group_id, block_slot[index]]
        half_of_rows = lax.dynamic_slice_in_dim(base_rows, (index * BLOCK).astype(jnp.int32), BLOCK, 0)
        cot_half = lax.dynamic_slice_in_dim(cotangent, (index * BLOCK).astype(jnp.int32), BLOCK, 0)
        in_panel = lax.dynamic_index_in_dim(in_all, expert, 0, keepdims=False)
        out_panel = lax.dynamic_index_in_dim(out_all, expert, 0, keepdims=False)
        gate_col = lax.dynamic_slice_in_dim(gating_weight_matrix, expert, 1, 1)
        rows_full = half_of_rows.astype(jnp.float32)
        cot_full = cot_half.astype(jnp.float32)
        rank_in = jnp.dot(half_of_rows, in_panel, preferred_element_type=jnp.float32)
        logit = jnp.dot(half_of_rows, gate_col, preferred_element_type=jnp.float32)
        tanh_full = jnp.tanh(rank_in)
        hyperbolic_half = tanh_full.astype(jnp.bfloat16)
        cross = jnp.dot(hyperbolic_half, out_panel.T, preferred_element_type=jnp.float32) + cross_bias[None, :]
        gate_prob = jax.nn.sigmoid(logit)
        scaled = live_flag * gate_prob
        gated_row_half = (scaled * rows_full * cot_full).astype(jnp.bfloat16)
        back_rank = jnp.dot(gated_row_half, out_panel, preferred_element_type=jnp.float32)
        gate_sum = jnp.sum(rows_full * cross * cot_full, axis=1, keepdims=True)
        gate_back = scaled * (1.0 - gate_prob) * gate_sum
        rank_gradient = (back_rank * (1.0 - tanh_full * tanh_full)).astype(jnp.bfloat16)
        d_rows = cot_full * (1.0 + scaled * cross)
        d_rows = d_rows + jnp.dot(rank_gradient, in_panel.T, preferred_element_type=jnp.float32)
        d_rows = d_rows + gate_back * gate_col.astype(jnp.float32).T
        add_out = jnp.dot(gated_row_half.T, hyperbolic_half, preferred_element_type=jnp.float32)
        add_in = jnp.dot(half_of_rows.T, rank_gradient, preferred_element_type=jnp.float32)
        grad_out = lax.dynamic_update_index_in_dim(grad_out, lax.dynamic_index_in_dim(grad_out, expert, 0, keepdims=False) + add_out, expert, 0)
        grad_in = lax.dynamic_update_index_in_dim(grad_in, lax.dynamic_index_in_dim(grad_in, expert, 0, keepdims=False) + add_in, expert, 0)
        return (grad_in, grad_out), d_rows.astype(jnp.bfloat16)

    start = (jnp.zeros((E, D, R), jnp.float32), jnp.zeros((E, D, R), jnp.float32))
    (grad_in, grad_out), d_blocks = lax.scan(step, start, jnp.arange(NBLK, dtype=jnp.int32))
    d_input = d_blocks.reshape(ROWS, D)
    d_in_panels = grad_in.reshape(E, MP_SLICES, SLICE, R).astype(jnp.bfloat16)
    d_out_panels = grad_out.reshape(E, MP_SLICES, SLICE, R).astype(jnp.bfloat16)
    return (d_input, d_in_panels, d_out_panels)
```

```python
import functools

import jax
import jax.numpy as jnp
from jax import lax
from jax.experimental import pallas as pl
from jax.experimental.pallas import tpu as pltpu
from jax.sharding import PartitionSpec as P

F32 = jnp.float32
BF16 = jnp.bfloat16
NT = (((1,), (1,)), ((), ()))
TN = (((0,), (0,)), ((), ()))
LOGIT, VPANEL, UPANEL, RANK, TANH, DOUT, BACK, RGRAD, GSUM, DIN = range(10)


def kernel(
    groups,
    mps,
    dev_ref,
    slot_ref,
    live_ref,
    code_ref,
    x_ref,
    g_ref,
    vin_ref,
    uin_ref,
    gate_ref,
    bias_ref,
    dx_ref,
    din_ref,
    dout_ref,
    vstage,
    ustage,
    vrecv,
    urecv,
    lsend,
    lrecv,
    rsend,
    rrecv,
    tanh_all,
    tanh_own,
    bsend,
    brecv,
    rgrad,
    qsend,
    qrecv,
    gated,
    dpart,
    osend,
    orecv,
    isend,
    irecv,
    send,
    recv,
):
    h = lax.axis_index("group")
    m = lax.axis_index("mp")
    experts, piece, rank = vin_ref.shape
    rows, width = x_ref.shape
    blocks = slot_ref.shape[0]
    block_rows = rows // blocks
    shard = rows // mps
    slots = dev_ref.shape[1]

    def offset(i, n):
        k = i // 2 + 1
        return (i % 2) * (n - 2 * k) + k

    def to_groups(which, src, dst):
        def step(i, carry):
            j = lax.rem(h + offset(i, groups), groups)
            pltpu.make_async_remote_copy(
                src_ref=src(j),
                dst_ref=dst,
                send_sem=send.at[which],
                recv_sem=recv.at[which],
                device_id={"group": j},
                device_id_type=pl.DeviceIdType.MESH,
            ).start()
            return carry

        lax.fori_loop(0, groups - 1, step, 0)

    def to_mps(which, src, dst):
        def step(i, carry):
            j = lax.rem(m + offset(i, mps), mps)
            pltpu.make_async_remote_copy(
                src_ref=src(j),
                dst_ref=dst,
                send_sem=send.at[which],
                recv_sem=recv.at[which],
                device_id={"mp": j},
                device_id_type=pl.DeviceIdType.MESH,
            ).start()
            return carry

        lax.fori_loop(0, mps - 1, step, 0)

    def drain(ref, sem):
        pltpu.make_async_copy(ref, ref, sem).wait()

    def block(b):
        return pl.ds(b * block_rows, block_rows)

    def part(j, size):
        return pl.ds(pl.multiple_of(j * size, size), size)

    def column(row):
        square = jnp.transpose(jnp.broadcast_to(row, (block_rows, block_rows)))
        return jnp.concatenate([square] * (width // block_rows), axis=1)

    barrier = pltpu.get_barrier_semaphore()

    for axis, me, n in (("group", h, groups), ("mp", m, mps)):

        def greet(i, carry, axis=axis, me=me, n=n):
            pl.semaphore_signal(
                barrier,
                inc=1,
                device_id={axis: lax.rem(me + i, n)},
                device_id_type=pl.DeviceIdType.MESH,
            )
            return carry

        lax.fori_loop(1, n, greet, 0)

    def stage(j, carry):
        for s in range(slots):
            e = dev_ref[j, s]
            vstage[j, s] = vin_ref[e]
            ustage[j, s] = uin_ref[e]
        return carry

    lax.fori_loop(0, groups, stage, 0)
    for s in range(slots):
        vrecv[s, part(h, piece), :] = vstage[h, s]
        urecv[s, part(h, piece), :] = ustage[h, s]

    slot_of = [slot_ref[b] for b in range(blocks)]
    gate_row = [gate_ref[dev_ref[h, slot_of[b]]] for b in range(blocks)]
    alive = [(live_ref[0] > b).astype(F32) for b in range(blocks)]
    which_row = lax.broadcasted_iota(jnp.int32, (8, block_rows), 0)
    logits = jnp.zeros((8, block_rows), F32)
    live_rows = jnp.zeros((8, block_rows), F32)
    for b in range(blocks):
        wide = jnp.broadcast_to(gate_row[b], (8, width)).astype(BF16)
        scores = lax.dot_general(wide, x_ref[block(b), :], NT, preferred_element_type=F32)
        logits = jnp.where(which_row == b, scores, logits)
        live_rows = jnp.where(which_row == b, alive[b], live_rows)
    lsend[...] = logits
    lrecv[m] = logits

    pl.semaphore_wait(barrier, groups + mps - 2)

    to_groups(VPANEL, lambda j: vstage.at[j], vrecv.at[:, part(h, piece), :])
    to_mps(LOGIT, lambda j: lsend, lrecv.at[m])
    drain(lrecv.at[pl.ds(0, mps - 1)], recv.at[LOGIT])
    prob = jax.nn.sigmoid(jnp.sum(lrecv[...], axis=0))
    scaled = live_rows * prob
    for b in range(blocks):
        gate = column(scaled[b : b + 1, :])
        gated[block(b), :] = (
            gate * x_ref[block(b), :].astype(F32) * g_ref[block(b), :].astype(F32)
        ).astype(BF16)

    drain(vrecv.at[:, pl.ds(0, width - piece), :], recv.at[VPANEL])
    to_groups(UPANEL, lambda j: ustage.at[j], urecv.at[:, part(h, piece), :])
    for b in range(blocks):
        rsend[block(b), :] = jnp.dot(
            x_ref[block(b), :], vrecv[slot_of[b]], preferred_element_type=F32
        ).astype(rsend.dtype)
    to_mps(RANK, lambda j: rsend.at[part(j, shard), :], rrecv.at[m])
    rrecv[m] = rsend[part(m, shard), :]
    drain(rrecv.at[pl.ds(0, mps - 1)], recv.at[RANK])
    tanh_full = jnp.tanh(jnp.sum(rrecv[...].astype(F32), axis=0))
    tanh_own[...] = tanh_full
    tanh_all[part(m, shard), :] = tanh_full.astype(BF16)
    mine = tanh_all.at[part(m, shard), :]
    to_mps(TANH, lambda j: mine, mine)
    drain(tanh_all.at[pl.ds(0, rows - shard), :], recv.at[TANH])

    def by_slot(value):
        parts = []
        for s in range(slots):
            held = [
                value[b * block_rows : (b + 1) * block_rows, :]
                * (slot_of[b] == s).astype(F32).astype(BF16)
                for b in range(blocks)
            ]
            parts.append(jnp.concatenate(held, axis=0))
        return parts

    for s, right in enumerate(by_slot(tanh_all[...])):
        osend[s] = lax.dot_general(gated[...], right, TN, preferred_element_type=F32).astype(
            osend.dtype
        )
    to_groups(DOUT, lambda j: osend.at[:, part(j, piece), :], orecv.at[h])
    orecv[h] = osend[:, part(h, piece), :]

    drain(urecv.at[:, pl.ds(0, width - piece), :], recv.at[UPANEL])
    for b in range(blocks):
        bsend[block(b), :] = jnp.dot(
            gated[block(b), :], urecv[slot_of[b]], preferred_element_type=F32
        ).astype(bsend.dtype)
    to_mps(BACK, lambda j: bsend.at[part(j, shard), :], brecv.at[m])
    brecv[m] = bsend[part(m, shard), :]

    sums = jnp.zeros((8, block_rows), F32)
    for b in range(blocks):
        cross = (
            lax.dot_general(
                tanh_all[block(b), :], urecv[slot_of[b]], NT, preferred_element_type=F32
            )
            + bias_ref[...]
        )
        gate = column(scaled[b : b + 1, :])
        full = g_ref[block(b), :].astype(F32)
        dpart[block(b), :] = full * (1.0 + gate * cross)
        product = x_ref[block(b), :].astype(F32) * cross * full
        folded = product[:, :block_rows]
        for c in range(1, width // block_rows):
            folded = folded + product[:, c * block_rows : (c + 1) * block_rows]
        row = jnp.sum(jnp.transpose(folded), axis=0, keepdims=True)
        sums = jnp.where(which_row == b, row, sums)
    qsend[...] = sums
    qrecv[m] = sums
    to_mps(GSUM, lambda j: qsend, qrecv.at[m])

    drain(brecv.at[pl.ds(0, mps - 1)], recv.at[BACK])
    back_rank = jnp.sum(brecv[...].astype(F32), axis=0)
    tanh_mine = tanh_own[...]
    rgrad[part(m, shard), :] = (back_rank * (1.0 - tanh_mine * tanh_mine)).astype(BF16)
    own = rgrad.at[part(m, shard), :]
    to_mps(RGRAD, lambda j: own, own)
    drain(rgrad.at[pl.ds(0, rows - shard), :], recv.at[RGRAD])
    for s, right in enumerate(by_slot(rgrad[...])):
        isend[s] = lax.dot_general(x_ref[...], right, TN, preferred_element_type=F32).astype(
            isend.dtype
        )
    to_groups(DIN, lambda j: isend.at[:, part(j, piece), :], irecv.at[h])
    irecv[h] = isend[:, part(h, piece), :]

    drain(qrecv.at[pl.ds(0, mps - 1)], recv.at[GSUM])
    gate_back = scaled * (1.0 - prob) * jnp.sum(qrecv[...], axis=0)
    for b in range(blocks):
        total = dpart[block(b), :] + lax.dot_general(
            rgrad[block(b), :], vrecv[slot_of[b]], NT, preferred_element_type=F32
        )
        total = total + column(gate_back[b : b + 1, :]) * gate_row[b]
        dx_ref[block(b), :] = total.astype(BF16)

    owners = (
        lax.broadcasted_iota(jnp.int32, (experts * piece, groups * slots * piece), 0)
        == code_ref[...]
    ).astype(F32).astype(BF16)

    def owner_sums(received, out):
        flat = received[...].reshape(groups * slots * piece, rank)
        total = jnp.dot(owners, flat, preferred_element_type=F32)
        out[...] = total.astype(BF16).reshape(experts, piece, rank)

    drain(orecv.at[pl.ds(0, groups - 1)], recv.at[DOUT])
    owner_sums(orecv, dout_ref)
    drain(irecv.at[pl.ds(0, groups - 1)], recv.at[DIN])
    owner_sums(irecv, din_ref)

    drain(vstage.at[pl.ds(0, groups - 1)], send.at[VPANEL])
    drain(ustage.at[pl.ds(0, groups - 1)], send.at[UPANEL])
    drain(orecv.at[pl.ds(0, groups - 1)], send.at[DOUT])
    drain(irecv.at[pl.ds(0, groups - 1)], send.at[DIN])
    drain(lrecv.at[pl.ds(0, mps - 1)], send.at[LOGIT])
    drain(qrecv.at[pl.ds(0, mps - 1)], send.at[GSUM])
    drain(rrecv.at[pl.ds(0, mps - 1)], send.at[RANK])
    drain(brecv.at[pl.ds(0, mps - 1)], send.at[BACK])
    drain(tanh_all.at[pl.ds(0, rows - shard), :], send.at[TANH])
    drain(rgrad.at[pl.ds(0, rows - shard), :], send.at[RGRAD])


def per_device(
    base_rows,
    cotangent,
    in_panels,
    out_panels,
    gating_weight_matrix,
    cross_bias,
    dev_experts,
    block_slot,
    live_blocks,
):
    groups = lax.axis_size("group")
    mps = lax.axis_size("mp")
    slots = dev_experts.shape[1]
    experts, _, piece, rank = in_panels.shape
    rows, width = base_rows.shape
    shard = rows // mps
    lanes = rows // block_slot.shape[0]
    gates = jnp.transpose(gating_weight_matrix).astype(F32).reshape(experts, 1, width)
    code = (
        dev_experts.reshape(groups * slots, 1) * piece + jnp.arange(piece, dtype=jnp.int32)[None, :]
    ).reshape(1, groups * slots * piece)
    vmem = pl.BlockSpec(memory_space=pltpu.VMEM)
    smem = pl.BlockSpec(memory_space=pltpu.SMEM)
    dx, din, dout = pl.pallas_call(
        functools.partial(kernel, groups, mps),
        out_shape=(
            jax.ShapeDtypeStruct((rows, width), BF16),
            jax.ShapeDtypeStruct((experts, piece, rank), BF16),
            jax.ShapeDtypeStruct((experts, piece, rank), BF16),
        ),
        in_specs=[smem] * 3 + [vmem] * 7,
        out_specs=(vmem, vmem, vmem),
        scratch_shapes=[
            pltpu.VMEM((groups, slots, piece, rank), BF16),
            pltpu.VMEM((groups, slots, piece, rank), BF16),
            pltpu.VMEM((slots, width, rank), BF16),
            pltpu.VMEM((slots, width, rank), BF16),
            pltpu.VMEM((8, lanes), F32),
            pltpu.VMEM((mps, 8, lanes), F32),
            pltpu.VMEM((rows, rank), BF16),
            pltpu.VMEM((mps, shard, rank), BF16),
            pltpu.VMEM((rows, rank), BF16),
            pltpu.VMEM((shard, rank), F32),
            pltpu.VMEM((rows, rank), BF16),
            pltpu.VMEM((mps, shard, rank), BF16),
            pltpu.VMEM((rows, rank), BF16),
            pltpu.VMEM((8, lanes), F32),
            pltpu.VMEM((mps, 8, lanes), F32),
            pltpu.VMEM((rows, width), BF16),
            pltpu.VMEM((rows, width), F32),
            pltpu.VMEM((slots, width, rank), BF16),
            pltpu.VMEM((groups, slots, piece, rank), BF16),
            pltpu.VMEM((slots, width, rank), BF16),
            pltpu.VMEM((groups, slots, piece, rank), BF16),
            pltpu.SemaphoreType.DMA((10,)),
            pltpu.SemaphoreType.DMA((10,)),
        ],
        compiler_params=pltpu.CompilerParams(
            collective_id=0, has_side_effects=True, vmem_limit_bytes=40 * 1024 * 1024
        ),
    )(
        dev_experts,
        block_slot,
        live_blocks,
        code,
        base_rows,
        cotangent,
        in_panels.reshape(experts, piece, rank),
        out_panels.reshape(experts, piece, rank),
        gates,
        cross_bias.reshape(1, width),
    )
    return (
        dx,
        din.reshape(experts, 1, piece, rank),
        dout.reshape(experts, 1, piece, rank),
    )


def solution(mesh):
    placed = (
        P("group", "mp"),
        P("group", "mp"),
        P(None, "mp", "group", None),
        P(None, "mp", "group", None),
        P("mp", None),
        P("mp"),
        P(),
        P("group"),
        P("group"),
    )
    return jax.shard_map(
        per_device,
        mesh=mesh,
        in_specs=placed,
        out_specs=(P("group", "mp"), P(None, "mp", "group", None), P(None, "mp", "group", None)),
        check_vma=False,
    )
```

```python
import functools

import jax
import jax.numpy as jnp
from jax import lax
from jax.experimental import pallas as pl
from jax.experimental.pallas import tpu as pltpu
from jax.sharding import PartitionSpec as P

F32 = jnp.float32
BF16 = jnp.bfloat16
NT = (((1,), (1,)), ((), ()))
TN = (((0,), (0,)), ((), ()))
LOGIT, VPANEL, UPANEL, RANK, TANH, DOUT, BACK, RGRAD, GSUM, DIN = range(10)
VIN, GATE, ROWS, COT, UIN, BIAS, DX_OUT, DIN_OUT, DOUT_OUT = range(9)


def kernel(
    groups,
    mps,
    dev_ref,
    slot_ref,
    live_ref,
    x_hbm,
    g_hbm,
    vin_hbm,
    uin_hbm,
    gate_hbm,
    bias_hbm,
    dx_hbm,
    din_hbm,
    dout_hbm,
    dx_ref,
    din_ref,
    dout_ref,
    x_ref,
    g_ref,
    vin_ref,
    uin_ref,
    gate_ref,
    bias_ref,
    owners,
    vstage,
    ustage,
    vrecv,
    urecv,
    lsend,
    lrecv,
    rsend,
    rrecv,
    tanh_all,
    tanh_own,
    bsend,
    brecv,
    rgrad,
    qsend,
    qrecv,
    gated,
    dpart,
    osend,
    orecv,
    isend,
    irecv,
    send,
    recv,
    local,
):
    h = lax.axis_index("group")
    m = lax.axis_index("mp")
    experts, piece, rank = vin_ref.shape
    rows, width = x_ref.shape
    blocks = slot_ref.shape[0]
    block_rows = rows // blocks
    shard = rows // mps
    slots = dev_ref.shape[0]

    def offset(i, n):
        k = i // 2 + 1
        return (i % 2) * (n - 2 * k) + k

    def to_groups(which, src, dst):
        def step(i, carry):
            k = groups // 2 - (i + 1) // 2
            j = lax.rem(h + (i % 2) * (groups - 2 * k) + k, groups)
            pltpu.make_async_remote_copy(
                src_ref=src(j),
                dst_ref=dst,
                send_sem=send.at[which],
                recv_sem=recv.at[which],
                device_id={"group": j},
                device_id_type=pl.DeviceIdType.MESH,
            ).start()
            return carry

        lax.fori_loop(0, groups - 1, step, 0)

    def to_mps(which, src, dst):
        def step(i, carry):
            j = lax.rem(m + offset(i, mps), mps)
            pltpu.make_async_remote_copy(
                src_ref=src(j),
                dst_ref=dst,
                send_sem=send.at[which],
                recv_sem=recv.at[which],
                device_id={"mp": j},
                device_id_type=pl.DeviceIdType.MESH,
            ).start()
            return carry

        lax.fori_loop(0, mps - 1, step, 0)

    def drain(ref, sem):
        pltpu.make_async_copy(ref, ref, sem).wait()

    def block(b):
        return pl.ds(b * block_rows, block_rows)

    def part(j, size):
        return pl.ds(pl.multiple_of(j * size, size), size)

    def column(row):
        square = jnp.transpose(jnp.broadcast_to(row, (block_rows, block_rows)))
        return jnp.concatenate([square] * (width // block_rows), axis=1)

    barrier = pltpu.get_barrier_semaphore()

    for axis, me, n in (("group", h, groups), ("mp", m, mps)):

        def greet(i, carry, axis=axis, me=me, n=n):
            pl.semaphore_signal(
                barrier,
                inc=1,
                device_id={axis: lax.rem(me + i, n)},
                device_id_type=pl.DeviceIdType.MESH,
            )
            return carry

        lax.fori_loop(1, n, greet, 0)

    loads = {
        which: pltpu.make_async_copy(src, dst, local.at[which])
        for which, src, dst in (
            (VIN, vin_hbm, vin_ref),
            (GATE, gate_hbm, gate_ref),
            (ROWS, x_hbm, x_ref),
            (UIN, uin_hbm, uin_ref),
            (COT, g_hbm, g_ref),
            (BIAS, bias_hbm, bias_ref),
        )
    }
    for load in loads.values():
        load.start()

    def stage_panels(panels, staged, received):
        def stage(j, carry):
            for s in range(slots):
                staged[j, s] = panels[dev_ref[s, j]]
            return carry

        lax.fori_loop(0, groups, stage, 0)
        for s in range(slots):
            received[s, part(h, piece), :] = staged[h, s]

    loads[VIN].wait()
    stage_panels(vin_ref, vstage, vrecv)
    pl.semaphore_wait(barrier, groups + mps - 2)
    to_groups(VPANEL, lambda j: vstage.at[j], vrecv.at[:, part(h, piece), :])
    loads[UIN].wait()
    stage_panels(uin_ref, ustage, urecv)
    to_groups(UPANEL, lambda j: ustage.at[j], urecv.at[:, part(h, piece), :])

    slot_of = [slot_ref[b] for b in range(blocks)]
    expert_of = [dev_ref[slot_of[b], h] for b in range(blocks)]
    alive = [(live_ref[0] > b).astype(F32) for b in range(blocks)]
    which_row = lax.broadcasted_iota(jnp.int32, (8, block_rows), 0)

    loads[GATE].wait()
    gate_lane = lax.broadcasted_iota(jnp.int32, (8, experts), 1)
    gate_sub = lax.broadcasted_iota(jnp.int32, (8, experts), 0)
    picks = jnp.zeros((8, experts), F32)
    for b in range(blocks):
        here = (gate_lane == expert_of[b]).astype(F32)
        picks = jnp.where(gate_sub == b, here, picks)
    gate_rows = jnp.dot(picks.astype(BF16), gate_ref[...], preferred_element_type=F32)
    loads[ROWS].wait()
    logits = jnp.zeros((8, block_rows), F32)
    live_rows = jnp.zeros((8, block_rows), F32)
    for b in range(blocks):
        scores = lax.dot_general(
            gate_rows.astype(BF16), x_ref[block(b), :], NT, preferred_element_type=F32
        )
        logits = jnp.where(which_row == b, scores, logits)
        live_rows = jnp.where(which_row == b, alive[b], live_rows)
    lsend[...] = logits
    lrecv[m] = logits

    to_mps(LOGIT, lambda j: lsend, lrecv.at[m])

    lane = lax.broadcasted_iota(jnp.int32, (1, groups * slots * piece), 1)

    def encode(j, code):
        for s in range(slots):
            code = code + (lane // piece == j * slots + s).astype(jnp.int32) * dev_ref[s, j] * piece
        return code

    code = lax.fori_loop(0, groups, encode, lane % piece)
    owners[...] = (
        (lax.broadcasted_iota(jnp.int32, owners.shape, 0) == code).astype(F32).astype(BF16)
    )
    loads[COT].wait()
    loads[BIAS].wait()
    drain(lrecv.at[pl.ds(0, mps - 1)], recv.at[LOGIT])
    prob = jax.nn.sigmoid(jnp.sum(lrecv[...], axis=0))
    scaled = live_rows * prob
    for b in range(blocks):
        gate = column(scaled[b : b + 1, :])
        gated[block(b), :] = (
            gate * x_ref[block(b), :].astype(F32) * g_ref[block(b), :].astype(F32)
        ).astype(BF16)

    drain(vrecv.at[:, pl.ds(0, width - piece), :], recv.at[VPANEL])
    for b in range(blocks):
        rsend[block(b), :] = jnp.dot(
            x_ref[block(b), :], vrecv[slot_of[b]], preferred_element_type=F32
        ).astype(rsend.dtype)
    to_mps(RANK, lambda j: rsend.at[part(j, shard), :], rrecv.at[m])
    rrecv[m] = rsend[part(m, shard), :]
    drain(rrecv.at[pl.ds(0, mps - 1)], recv.at[RANK])
    tanh_full = jnp.tanh(jnp.sum(rrecv[...].astype(F32), axis=0))
    tanh_own[...] = tanh_full
    tanh_all[part(m, shard), :] = tanh_full.astype(BF16)
    mine = tanh_all.at[part(m, shard), :]
    to_mps(TANH, lambda j: mine, mine)
    drain(tanh_all.at[pl.ds(0, rows - shard), :], recv.at[TANH])

    def by_slot(value):
        parts = []
        for s in range(slots):
            held = [
                value[b * block_rows : (b + 1) * block_rows, :]
                * (slot_of[b] == s).astype(F32).astype(BF16)
                for b in range(blocks)
            ]
            parts.append(jnp.concatenate(held, axis=0))
        return parts

    for s, right in enumerate(by_slot(tanh_all[...])):
        osend[s] = lax.dot_general(gated[...], right, TN, preferred_element_type=F32).astype(
            osend.dtype
        )
    to_groups(DOUT, lambda j: osend.at[:, part(j, piece), :], orecv.at[h])
    orecv[h] = osend[:, part(h, piece), :]

    drain(urecv.at[:, pl.ds(0, width - piece), :], recv.at[UPANEL])
    for b in range(blocks):
        bsend[block(b), :] = jnp.dot(
            gated[block(b), :], urecv[slot_of[b]], preferred_element_type=F32
        ).astype(bsend.dtype)
    to_mps(BACK, lambda j: bsend.at[part(j, shard), :], brecv.at[m])
    brecv[m] = bsend[part(m, shard), :]

    sums = jnp.zeros((8, block_rows), F32)
    for b in range(blocks):
        cross = (
            lax.dot_general(
                tanh_all[block(b), :], urecv[slot_of[b]], NT, preferred_element_type=F32
            )
            + bias_ref[...]
        )
        gate = column(scaled[b : b + 1, :])
        full = g_ref[block(b), :].astype(F32)
        dpart[block(b), :] = full * (1.0 + gate * cross)
        product = x_ref[block(b), :].astype(F32) * cross * full
        folded = product[:, :block_rows]
        for c in range(1, width // block_rows):
            folded = folded + product[:, c * block_rows : (c + 1) * block_rows]
        row = jnp.sum(jnp.transpose(folded), axis=0, keepdims=True)
        sums = jnp.where(which_row == b, row, sums)
    qsend[...] = sums
    qrecv[m] = sums
    to_mps(GSUM, lambda j: qsend, qrecv.at[m])

    drain(brecv.at[pl.ds(0, mps - 1)], recv.at[BACK])
    back_rank = jnp.sum(brecv[...].astype(F32), axis=0)
    tanh_mine = tanh_own[...]
    rgrad[part(m, shard), :] = (back_rank * (1.0 - tanh_mine * tanh_mine)).astype(BF16)
    own = rgrad.at[part(m, shard), :]
    to_mps(RGRAD, lambda j: own, own)
    drain(rgrad.at[pl.ds(0, rows - shard), :], recv.at[RGRAD])
    for s, right in enumerate(by_slot(rgrad[...])):
        isend[s] = lax.dot_general(x_ref[...], right, TN, preferred_element_type=F32).astype(
            isend.dtype
        )
    to_groups(DIN, lambda j: isend.at[:, part(j, piece), :], irecv.at[h])
    irecv[h] = isend[:, part(h, piece), :]

    drain(qrecv.at[pl.ds(0, mps - 1)], recv.at[GSUM])
    gate_back = scaled * (1.0 - prob) * jnp.sum(qrecv[...], axis=0)
    for b in range(blocks):
        total = dpart[block(b), :] + lax.dot_general(
            rgrad[block(b), :], vrecv[slot_of[b]], NT, preferred_element_type=F32
        )
        total = total + column(gate_back[b : b + 1, :]) * gate_rows[b : b + 1, :]
        dx_ref[block(b), :] = total.astype(BF16)

    stores = {
        which: pltpu.make_async_copy(src, dst, local.at[which])
        for which, src, dst in (
            (DX_OUT, dx_ref, dx_hbm),
            (DIN_OUT, din_ref, din_hbm.at[:, 0]),
            (DOUT_OUT, dout_ref, dout_hbm.at[:, 0]),
        )
    }
    stores[DX_OUT].start()

    def owner_sums(received, out):
        flat = received[...].reshape(groups * slots * piece, rank)
        total = jnp.dot(owners[...], flat, preferred_element_type=F32)
        out[...] = total.astype(BF16).reshape(experts, piece, rank)

    drain(orecv.at[pl.ds(0, groups - 1)], recv.at[DOUT])
    owner_sums(orecv, dout_ref)
    stores[DOUT_OUT].start()
    drain(irecv.at[pl.ds(0, groups - 1)], recv.at[DIN])
    owner_sums(irecv, din_ref)
    stores[DIN_OUT].start()

    drain(vstage.at[pl.ds(0, groups - 1)], send.at[VPANEL])
    drain(ustage.at[pl.ds(0, groups - 1)], send.at[UPANEL])
    drain(orecv.at[pl.ds(0, groups - 1)], send.at[DOUT])
    drain(irecv.at[pl.ds(0, groups - 1)], send.at[DIN])
    drain(lrecv.at[pl.ds(0, mps - 1)], send.at[LOGIT])
    drain(qrecv.at[pl.ds(0, mps - 1)], send.at[GSUM])
    drain(rrecv.at[pl.ds(0, mps - 1)], send.at[RANK])
    drain(brecv.at[pl.ds(0, mps - 1)], send.at[BACK])
    drain(tanh_all.at[pl.ds(0, rows - shard), :], send.at[TANH])
    drain(rgrad.at[pl.ds(0, rows - shard), :], send.at[RGRAD])
    for store in stores.values():
        store.wait()


def write_out(*refs):
    sources, targets, held = refs[0:3], refs[3:6], refs[6:9]
    came, went = refs[9:]
    loads = [pltpu.make_async_copy(sources[i], held[i], came.at[i]) for i in range(3)]
    stores = [pltpu.make_async_copy(held[i], targets[i], went.at[i]) for i in range(3)]
    for load in loads:
        load.start()
    for load, store in zip(loads, stores):
        load.wait()
        store.start()
    for store in stores:
        store.wait()


def per_device(
    base_rows,
    cotangent,
    in_panels,
    out_panels,
    gating_weight_matrix,
    cross_bias,
    dev_experts,
    block_slot,
    live_blocks,
):
    groups = lax.axis_size("group")
    mps = lax.axis_size("mp")
    slots = dev_experts.shape[1]
    experts, _, piece, rank = in_panels.shape
    rows, width = base_rows.shape
    shard = rows // mps
    lanes = rows // block_slot.shape[0]
    smem = pl.BlockSpec(memory_space=pltpu.SMEM)
    hbm = pl.BlockSpec(memory_space=pltpu.HBM)
    results = pl.pallas_call(
        functools.partial(kernel, groups, mps),
        out_shape=(
            jax.ShapeDtypeStruct((rows, width), BF16),
            jax.ShapeDtypeStruct((experts, 1, piece, rank), BF16),
            jax.ShapeDtypeStruct((experts, 1, piece, rank), BF16),
        ),
        in_specs=[smem] * 3 + [hbm] * 6,
        out_specs=(hbm, hbm, hbm),
        scratch_shapes=[
            pltpu.VMEM((rows, width), BF16),
            pltpu.VMEM((experts, piece, rank), BF16),
            pltpu.VMEM((experts, piece, rank), BF16),
            pltpu.VMEM((rows, width), BF16),
            pltpu.VMEM((rows, width), BF16),
            pltpu.VMEM((experts, piece, rank), BF16),
            pltpu.VMEM((experts, piece, rank), BF16),
            pltpu.VMEM((experts, width), BF16),
            pltpu.VMEM((1, width), F32),
            pltpu.VMEM((experts * piece, groups * slots * piece), BF16),
            pltpu.VMEM((groups, slots, piece, rank), BF16),
            pltpu.VMEM((groups, slots, piece, rank), BF16),
            pltpu.VMEM((slots, width, rank), BF16),
            pltpu.VMEM((slots, width, rank), BF16),
            pltpu.VMEM((8, lanes), F32),
            pltpu.VMEM((mps, 8, lanes), F32),
            pltpu.VMEM((rows, rank), BF16),
            pltpu.VMEM((mps, shard, rank), BF16),
            pltpu.VMEM((rows, rank), BF16),
            pltpu.VMEM((shard, rank), F32),
            pltpu.VMEM((rows, rank), BF16),
            pltpu.VMEM((mps, shard, rank), BF16),
            pltpu.VMEM((rows, rank), BF16),
            pltpu.VMEM((8, lanes), F32),
            pltpu.VMEM((mps, 8, lanes), F32),
            pltpu.VMEM((rows, width), BF16),
            pltpu.VMEM((rows, width), F32),
            pltpu.VMEM((slots, width, rank), BF16),
            pltpu.VMEM((groups, slots, piece, rank), BF16),
            pltpu.VMEM((slots, width, rank), BF16),
            pltpu.VMEM((groups, slots, piece, rank), BF16),
            pltpu.SemaphoreType.DMA((10,)),
            pltpu.SemaphoreType.DMA((10,)),
            pltpu.SemaphoreType.DMA((9,)),
        ],
        compiler_params=pltpu.CompilerParams(
            collective_id=0, has_side_effects=True, vmem_limit_bytes=60 * 1024 * 1024
        ),
    )(
        jnp.transpose(dev_experts),
        block_slot,
        live_blocks,
        base_rows,
        cotangent,
        in_panels.reshape(experts, piece, rank),
        out_panels.reshape(experts, piece, rank),
        jnp.transpose(gating_weight_matrix),
        cross_bias.reshape(1, width),
    )
    return pl.pallas_call(
        write_out,
        out_shape=tuple(jax.ShapeDtypeStruct(a.shape, a.dtype) for a in results),
        in_specs=[hbm] * 3,
        out_specs=(hbm, hbm, hbm),
        scratch_shapes=[pltpu.VMEM(a.shape, a.dtype) for a in results]
        + [pltpu.SemaphoreType.DMA((3,)), pltpu.SemaphoreType.DMA((3,))],
        compiler_params=pltpu.CompilerParams(vmem_limit_bytes=60 * 1024 * 1024),
    )(*results)


def solution(mesh):
    placed = (
        P("group", "mp"),
        P("group", "mp"),
        P(None, "mp", "group", None),
        P(None, "mp", "group", None),
        P("mp", None),
        P("mp"),
        P(),
        P("group"),
        P("group"),
    )
    return jax.shard_map(
        per_device,
        mesh=mesh,
        in_specs=placed,
        out_specs=(P("group", "mp"), P(None, "mp", "group", None), P(None, "mp", "group", None)),
        check_vma=False,
    )
```

```python
import functools

import jax
import jax.numpy as jnp
from jax import lax
from jax.experimental import pallas as pl
from jax.experimental.pallas import tpu as pltpu
from jax.sharding import PartitionSpec as P

F32 = jnp.float32
BF16 = jnp.bfloat16
NT = (((1,), (1,)), ((), ()))
TN = (((0,), (0,)), ((), ()))
HALVES = 2
LOGIT, GSUM, DOUT, DIN = range(4)
VPANEL, UPANEL, RANK, TANH, BACK, RGRAD = range(4, 4 + 6 * HALVES, HALVES)
VIN, GATE, ROWS, COT, UIN, BIAS, DX_OUT, DIN_OUT, DOUT_OUT = range(9)


def kernel(
    groups,
    mps,
    dev_ref,
    slot_ref,
    live_ref,
    x_hbm,
    g_hbm,
    vin_hbm,
    uin_hbm,
    gate_hbm,
    bias_hbm,
    dx_hbm,
    din_hbm,
    dout_hbm,
    dx_ref,
    din_ref,
    dout_ref,
    x_ref,
    g_ref,
    vin_ref,
    uin_ref,
    gate_ref,
    bias_ref,
    owners,
    vstage,
    ustage,
    vfirst,
    vsecond,
    ufirst,
    usecond,
    lsend,
    lrecv,
    rsend,
    rrecv,
    tanh_all,
    tanh_own,
    bsend,
    brecv,
    rgrad,
    qsend,
    qrecv,
    gated,
    dpart,
    osend,
    orecv,
    isend,
    irecv,
    send,
    recv,
    local,
):
    h = lax.axis_index("group")
    m = lax.axis_index("mp")
    experts, piece, rank = vin_ref.shape
    rows, width = x_ref.shape
    blocks = slot_ref.shape[0]
    block_rows = rows // blocks
    shard = rows // mps
    slots = dev_ref.shape[0]
    half = rank // HALVES
    vrecv, urecv = (vfirst, vsecond), (ufirst, usecond)

    def offset(i, n):
        k = i // 2 + 1
        return (i % 2) * (n - 2 * k) + k

    def to_groups(which, src, dst):
        def step(i, carry):
            k = groups // 2 - (i + 1) // 2
            j = lax.rem(h + (i % 2) * (groups - 2 * k) + k, groups)
            pltpu.make_async_remote_copy(
                src_ref=src(j),
                dst_ref=dst,
                send_sem=send.at[which],
                recv_sem=recv.at[which],
                device_id={"group": j},
                device_id_type=pl.DeviceIdType.MESH,
            ).start()
            return carry

        lax.fori_loop(0, groups - 1, step, 0)

    def to_mps(which, src, dst):
        def step(i, carry):
            j = lax.rem(m + offset(i, mps), mps)
            pltpu.make_async_remote_copy(
                src_ref=src(j),
                dst_ref=dst,
                send_sem=send.at[which],
                recv_sem=recv.at[which],
                device_id={"mp": j},
                device_id_type=pl.DeviceIdType.MESH,
            ).start()
            return carry

        lax.fori_loop(0, mps - 1, step, 0)

    def drain(ref, sem):
        pltpu.make_async_copy(ref, ref, sem).wait()

    def block(b):
        return pl.ds(b * block_rows, block_rows)

    def part(j, size):
        return pl.ds(pl.multiple_of(j * size, size), size)

    def column(row):
        square = jnp.transpose(jnp.broadcast_to(row, (block_rows, block_rows)))
        return jnp.concatenate([square] * (width // block_rows), axis=1)

    barrier = pltpu.get_barrier_semaphore()

    for axis, me, n in (("group", h, groups), ("mp", m, mps)):

        def greet(i, carry, axis=axis, me=me, n=n):
            pl.semaphore_signal(
                barrier,
                inc=1,
                device_id={axis: lax.rem(me + i, n)},
                device_id_type=pl.DeviceIdType.MESH,
            )
            return carry

        lax.fori_loop(1, n, greet, 0)

    loads = {
        which: pltpu.make_async_copy(src, dst, local.at[which])
        for which, src, dst in (
            (VIN, vin_hbm, vin_ref),
            (GATE, gate_hbm, gate_ref),
            (ROWS, x_hbm, x_ref),
            (UIN, uin_hbm, uin_ref),
            (COT, g_hbm, g_ref),
            (BIAS, bias_hbm, bias_ref),
        )
    }
    for load in loads.values():
        load.start()

    def stage_panels(panels, staged, received):
        def stage(j, carry):
            for s in range(slots):
                panel = panels[dev_ref[s, j]]
                for a in range(HALVES):
                    staged[a, j, s] = panel[:, a * half : (a + 1) * half]
            return carry

        lax.fori_loop(0, groups, stage, 0)
        for a in range(HALVES):
            for s in range(slots):
                received[a][s, part(h, piece), :] = staged[a, h, s]

    def send_panels(which, staged, received):
        for a in range(HALVES):
            to_groups(
                which + a, lambda j, a=a: staged.at[a, j], received[a].at[:, part(h, piece), :]
            )

    def await_panel(which, a, received):
        drain(received[a].at[:, pl.ds(0, width - piece), :], recv.at[which + a])

    loads[VIN].wait()
    stage_panels(vin_ref, vstage, vrecv)
    pl.semaphore_wait(barrier, groups + mps - 2)
    send_panels(VPANEL, vstage, vrecv)
    loads[UIN].wait()
    stage_panels(uin_ref, ustage, urecv)
    send_panels(UPANEL, ustage, urecv)

    slot_of = [slot_ref[b] for b in range(blocks)]
    expert_of = [dev_ref[slot_of[b], h] for b in range(blocks)]
    alive = [(live_ref[0] > b).astype(F32) for b in range(blocks)]
    which_row = lax.broadcasted_iota(jnp.int32, (8, block_rows), 0)

    loads[GATE].wait()
    gate_lane = lax.broadcasted_iota(jnp.int32, (8, experts), 1)
    gate_sub = lax.broadcasted_iota(jnp.int32, (8, experts), 0)
    picks = jnp.zeros((8, experts), F32)
    for b in range(blocks):
        here = (gate_lane == expert_of[b]).astype(F32)
        picks = jnp.where(gate_sub == b, here, picks)
    gate_rows = jnp.dot(picks.astype(BF16), gate_ref[...], preferred_element_type=F32)
    loads[ROWS].wait()
    logits = jnp.zeros((8, block_rows), F32)
    live_rows = jnp.zeros((8, block_rows), F32)
    for b in range(blocks):
        scores = lax.dot_general(
            gate_rows.astype(BF16), x_ref[block(b), :], NT, preferred_element_type=F32
        )
        logits = jnp.where(which_row == b, scores, logits)
        live_rows = jnp.where(which_row == b, alive[b], live_rows)
    lsend[...] = logits
    lrecv[m] = logits

    to_mps(LOGIT, lambda j: lsend, lrecv.at[m])

    lane = lax.broadcasted_iota(jnp.int32, (1, groups * slots * piece), 1)

    def encode(j, code):
        for s in range(slots):
            code = code + (lane // piece == j * slots + s).astype(jnp.int32) * dev_ref[s, j] * piece
        return code

    code = lax.fori_loop(0, groups, encode, lane % piece)
    owners[...] = (
        (lax.broadcasted_iota(jnp.int32, owners.shape, 0) == code).astype(F32).astype(BF16)
    )
    loads[COT].wait()
    loads[BIAS].wait()
    drain(lrecv.at[pl.ds(0, mps - 1)], recv.at[LOGIT])
    prob = jax.nn.sigmoid(jnp.sum(lrecv[...], axis=0))
    scaled = live_rows * prob
    for b in range(blocks):
        gate = column(scaled[b : b + 1, :])
        gated[block(b), :] = (
            gate * x_ref[block(b), :].astype(F32) * g_ref[block(b), :].astype(F32)
        ).astype(BF16)

    def exchange(which, a, left, panels, sent, received):
        for b in range(blocks):
            sent[a, block(b), :] = jnp.dot(
                left[block(b), :], panels[a][slot_of[b]], preferred_element_type=F32
            )
        to_mps(which + a, lambda j: sent.at[a, part(j, shard), :], received.at[a, m])
        received[a, m] = sent[a, part(m, shard), :]

    def total(which, a, received):
        drain(received.at[a, pl.ds(0, mps - 1)], recv.at[which + a])
        return jnp.sum(received[a], axis=0)

    def share(which, a, gathered, value):
        gathered[a, part(m, shard), :] = value.astype(BF16)
        mine = gathered.at[a, part(m, shard), :]
        to_mps(which + a, lambda j: mine, mine)

    def await_shared(which, gathered):
        for a in range(HALVES):
            drain(gathered.at[a, pl.ds(0, rows - shard), :], recv.at[which + a])
        return jnp.concatenate([gathered[a] for a in range(HALVES)], axis=1)

    for a in range(HALVES):
        await_panel(VPANEL, a, vrecv)
        exchange(RANK, a, x_ref, vrecv, rsend, rrecv)
        tanh_full = jnp.tanh(total(RANK, a, rrecv))
        tanh_own[a] = tanh_full
        share(TANH, a, tanh_all, tanh_full)

    def share_rank_back(a):
        back_rank = total(BACK, a, brecv)
        tanh_mine = tanh_own[a]
        share(RGRAD, a, rgrad, back_rank * (1.0 - tanh_mine * tanh_mine))

    await_panel(UPANEL, 0, urecv)
    exchange(BACK, 0, gated, urecv, bsend, brecv)

    def by_slot(value):
        parts = []
        for s in range(slots):
            held = [
                value[b * block_rows : (b + 1) * block_rows, :]
                * (slot_of[b] == s).astype(F32).astype(BF16)
                for b in range(blocks)
            ]
            parts.append(jnp.concatenate(held, axis=0))
        return parts

    for s, right in enumerate(by_slot(await_shared(TANH, tanh_all))):
        osend[s] = lax.dot_general(gated[...], right, TN, preferred_element_type=F32).astype(
            osend.dtype
        )
    to_groups(DOUT, lambda j: osend.at[:, part(j, piece), :], orecv.at[h])
    orecv[h] = osend[:, part(h, piece), :]

    share_rank_back(0)
    for a in range(1, HALVES):
        await_panel(UPANEL, a, urecv)
        exchange(BACK, a, gated, urecv, bsend, brecv)

    def back_to_width(left, panels, b):
        return sum(
            lax.dot_general(
                left[a, block(b), :], panels[a][slot_of[b]], NT, preferred_element_type=F32
            )
            for a in range(HALVES)
        )

    sums = jnp.zeros((8, block_rows), F32)
    for b in range(blocks):
        cross = back_to_width(tanh_all, urecv, b) + bias_ref[...]
        gate = column(scaled[b : b + 1, :])
        full = g_ref[block(b), :].astype(F32)
        dpart[block(b), :] = full * (1.0 + gate * cross)
        product = x_ref[block(b), :].astype(F32) * cross * full
        folded = product[:, :block_rows]
        for c in range(1, width // block_rows):
            folded = folded + product[:, c * block_rows : (c + 1) * block_rows]
        row = jnp.sum(jnp.transpose(folded), axis=0, keepdims=True)
        sums = jnp.where(which_row == b, row, sums)
    qsend[...] = sums
    qrecv[m] = sums
    to_mps(GSUM, lambda j: qsend, qrecv.at[m])

    for a in range(1, HALVES):
        share_rank_back(a)
    for s, right in enumerate(by_slot(await_shared(RGRAD, rgrad))):
        isend[s] = lax.dot_general(x_ref[...], right, TN, preferred_element_type=F32).astype(
            isend.dtype
        )
    to_groups(DIN, lambda j: isend.at[:, part(j, piece), :], irecv.at[h])
    irecv[h] = isend[:, part(h, piece), :]

    drain(qrecv.at[pl.ds(0, mps - 1)], recv.at[GSUM])
    gate_back = scaled * (1.0 - prob) * jnp.sum(qrecv[...], axis=0)
    for b in range(blocks):
        d_rows = dpart[block(b), :] + back_to_width(rgrad, vrecv, b)
        d_rows = d_rows + column(gate_back[b : b + 1, :]) * gate_rows[b : b + 1, :]
        dx_ref[block(b), :] = d_rows.astype(BF16)

    stores = {
        which: pltpu.make_async_copy(src, dst, local.at[which])
        for which, src, dst in (
            (DX_OUT, dx_ref, dx_hbm),
            (DIN_OUT, din_ref, din_hbm.at[:, 0]),
            (DOUT_OUT, dout_ref, dout_hbm.at[:, 0]),
        )
    }
    stores[DX_OUT].start()

    def owner_sums(received, out):
        flat = received[...].reshape(groups * slots * piece, rank)
        total = jnp.dot(owners[...], flat, preferred_element_type=F32)
        out[...] = total.astype(BF16).reshape(experts, piece, rank)

    drain(orecv.at[pl.ds(0, groups - 1)], recv.at[DOUT])
    owner_sums(orecv, dout_ref)
    stores[DOUT_OUT].start()
    drain(irecv.at[pl.ds(0, groups - 1)], recv.at[DIN])
    owner_sums(irecv, din_ref)
    stores[DIN_OUT].start()

    for a in range(HALVES):
        drain(vstage.at[a, pl.ds(0, groups - 1)], send.at[VPANEL + a])
        drain(ustage.at[a, pl.ds(0, groups - 1)], send.at[UPANEL + a])
        drain(rrecv.at[a, pl.ds(0, mps - 1)], send.at[RANK + a])
        drain(brecv.at[a, pl.ds(0, mps - 1)], send.at[BACK + a])
        drain(tanh_all.at[a, pl.ds(0, rows - shard), :], send.at[TANH + a])
        drain(rgrad.at[a, pl.ds(0, rows - shard), :], send.at[RGRAD + a])
    drain(orecv.at[pl.ds(0, groups - 1)], send.at[DOUT])
    drain(irecv.at[pl.ds(0, groups - 1)], send.at[DIN])
    drain(lrecv.at[pl.ds(0, mps - 1)], send.at[LOGIT])
    drain(qrecv.at[pl.ds(0, mps - 1)], send.at[GSUM])
    for store in stores.values():
        store.wait()


def write_out(*refs):
    sources, targets, held = refs[0:3], refs[3:6], refs[6:9]
    came, went = refs[9:]
    loads = [pltpu.make_async_copy(sources[i], held[i], came.at[i]) for i in range(3)]
    stores = [pltpu.make_async_copy(held[i], targets[i], went.at[i]) for i in range(3)]
    for load in loads:
        load.start()
    for load, store in zip(loads, stores):
        load.wait()
        store.start()
    for store in stores:
        store.wait()


def per_device(
    base_rows,
    cotangent,
    in_panels,
    out_panels,
    gating_weight_matrix,
    cross_bias,
    dev_experts,
    block_slot,
    live_blocks,
):
    groups = lax.axis_size("group")
    mps = lax.axis_size("mp")
    slots = dev_experts.shape[1]
    experts, _, piece, rank = in_panels.shape
    rows, width = base_rows.shape
    shard = rows // mps
    lanes = rows // block_slot.shape[0]
    smem = pl.BlockSpec(memory_space=pltpu.SMEM)
    hbm = pl.BlockSpec(memory_space=pltpu.HBM)
    results = pl.pallas_call(
        functools.partial(kernel, groups, mps),
        out_shape=(
            jax.ShapeDtypeStruct((rows, width), BF16),
            jax.ShapeDtypeStruct((experts, 1, piece, rank), BF16),
            jax.ShapeDtypeStruct((experts, 1, piece, rank), BF16),
        ),
        in_specs=[smem] * 3 + [hbm] * 6,
        out_specs=(hbm, hbm, hbm),
        scratch_shapes=[
            pltpu.VMEM((rows, width), BF16),
            pltpu.VMEM((experts, piece, rank), BF16),
            pltpu.VMEM((experts, piece, rank), BF16),
            pltpu.VMEM((rows, width), BF16),
            pltpu.VMEM((rows, width), BF16),
            pltpu.VMEM((experts, piece, rank), BF16),
            pltpu.VMEM((experts, piece, rank), BF16),
            pltpu.VMEM((experts, width), BF16),
            pltpu.VMEM((1, width), F32),
            pltpu.VMEM((experts * piece, groups * slots * piece), BF16),
            pltpu.VMEM((HALVES, groups, slots, piece, rank // HALVES), BF16),
            pltpu.VMEM((HALVES, groups, slots, piece, rank // HALVES), BF16),
            pltpu.VMEM((slots, width, rank // HALVES), BF16),
            pltpu.VMEM((slots, width, rank // HALVES), BF16),
            pltpu.VMEM((slots, width, rank // HALVES), BF16),
            pltpu.VMEM((slots, width, rank // HALVES), BF16),
            pltpu.VMEM((8, lanes), F32),
            pltpu.VMEM((mps, 8, lanes), F32),
            pltpu.VMEM((HALVES, rows, rank // HALVES), F32),
            pltpu.VMEM((HALVES, mps, shard, rank // HALVES), F32),
            pltpu.VMEM((HALVES, rows, rank // HALVES), BF16),
            pltpu.VMEM((HALVES, shard, rank // HALVES), F32),
            pltpu.VMEM((HALVES, rows, rank // HALVES), F32),
            pltpu.VMEM((HALVES, mps, shard, rank // HALVES), F32),
            pltpu.VMEM((HALVES, rows, rank // HALVES), BF16),
            pltpu.VMEM((8, lanes), F32),
            pltpu.VMEM((mps, 8, lanes), F32),
            pltpu.VMEM((rows, width), BF16),
            pltpu.VMEM((rows, width), F32),
            pltpu.VMEM((slots, width, rank), BF16),
            pltpu.VMEM((groups, slots, piece, rank), BF16),
            pltpu.VMEM((slots, width, rank), BF16),
            pltpu.VMEM((groups, slots, piece, rank), BF16),
            pltpu.SemaphoreType.DMA((4 + 6 * HALVES,)),
            pltpu.SemaphoreType.DMA((4 + 6 * HALVES,)),
            pltpu.SemaphoreType.DMA((9,)),
        ],
        compiler_params=pltpu.CompilerParams(
            collective_id=0, has_side_effects=True, vmem_limit_bytes=60 * 1024 * 1024
        ),
    )(
        jnp.transpose(dev_experts),
        block_slot,
        live_blocks,
        base_rows,
        cotangent,
        in_panels.reshape(experts, piece, rank),
        out_panels.reshape(experts, piece, rank),
        jnp.transpose(gating_weight_matrix),
        cross_bias.reshape(1, width),
    )
    return pl.pallas_call(
        write_out,
        out_shape=tuple(jax.ShapeDtypeStruct(a.shape, a.dtype) for a in results),
        in_specs=[hbm] * 3,
        out_specs=(hbm, hbm, hbm),
        scratch_shapes=[pltpu.VMEM(a.shape, a.dtype) for a in results]
        + [pltpu.SemaphoreType.DMA((3,)), pltpu.SemaphoreType.DMA((3,))],
        compiler_params=pltpu.CompilerParams(vmem_limit_bytes=60 * 1024 * 1024),
    )(*results)


def solution(mesh):
    placed = (
        P("group", "mp"),
        P("group", "mp"),
        P(None, "mp", "group", None),
        P(None, "mp", "group", None),
        P("mp", None),
        P("mp"),
        P(),
        P("group"),
        P("group"),
    )
    return jax.shard_map(
        per_device,
        mesh=mesh,
        in_specs=placed,
        out_specs=(P("group", "mp"), P(None, "mp", "group", None), P(None, "mp", "group", None)),
        check_vma=False,
    )
```
